1024 devices in a mesh: row: 64 (over z, x), col: 16 (over y, core).
Axes of the slice: x: 8, y: 8, z: 8, core: 2. Of those that a mesh axis runs over, the one named last changes fastest.
Arguments:
- features: bfloat16 [65536, 256], P(('row', 'col')), may hold values from -6 to 6
- tiles: bfloat16 [64, 16, 96, 128, 128], P('row', 'col'), may hold values from -0.0546875 to 0.0546875
- places: int32 [64, 16, 96], P('row', 'col'), may hold values from 0 to 255, as said below
- counts: int32 [64, 16], P('row', 'col'), may hold values from 24 to 96, as said below
- weight: bfloat16 [256, 256], replicated, may hold values from -0.375 to 0.375
Outputs:
- hidden_out: bfloat16 [65536, 256], P(('row', 'col'))
The draws below stay inside these ranges and needn't reach their ends.
Inputs may be any that keep to these rules, and one draw needn't show every extreme that they name: `places`: slots below counts of a device hold its occupied tile positions, distinct and increasing; the other slots hold distinct unoccupied positions. `counts`: some device holds exactly 96 occupied tiles and some exactly 24.
All inputs are finite; a program needn't handle non-finite values.
Results may differ from the reference program's by a relative error of at most 0.0049.
Values may be sent and summed in bfloat16 or wider, within the bound.
A program may use at most 64 MiB of HBM per device.

```python
import jax
import jax.numpy as jnp
from jax import lax

F = 256
TILE = 128
MAST = 64
VERTICES = 65536
SLOTS = 256
KMAX = 96
N_ROW = 64
N_COL = 16


def shared_counts(key):
    key = jax.random.fold_in(key, 11)
    first_key, second_key, third_key = jax.random.split(key, 3)
    span = KMAX - KMAX // 4
    drawn = jax.random.randint(first_key, (N_ROW * N_COL,), 0, span + 1)
    values = KMAX // 4 + drawn * drawn // max(span, 1)
    devices = N_ROW * N_COL
    highest = jax.random.randint(second_key, (), 0, devices)
    lowest = (highest + 1 + jax.random.randint(third_key, (), 0, devices - 1)) % devices
    values = values.at[highest].set(KMAX).at[lowest].set(KMAX // 4)
    return values.reshape(N_ROW, N_COL).astype(jnp.int32)


def draw_counts(key, part):
    shared = shared_counts(key)
    return shared


def draw_places(key, part):
    shared = shared_counts(key)
    key = jax.random.fold_in(key, 5)
    keys = jax.random.split(key, N_ROW * N_COL)
    orders = jax.vmap(lambda single: jax.random.permutation(single, SLOTS))(keys).reshape(N_ROW, N_COL, SLOTS)
    indices = jnp.arange(SLOTS, dtype=jnp.int32)
    sortkey = jnp.where(indices[None, None, :] < shared[:, :, None], orders, orders + SLOTS)
    ordered = jnp.sort(sortkey, axis=-1)[:, :, :KMAX]
    return (ordered % SLOTS).astype(jnp.int32)


def block_levels(rng, shape, shards, smallest, high):
    gain, own = 1.0, jax.random.fold_in(rng, 6)
    for axis_at, blocks in shards:
        steps = jnp.exp(jax.random.uniform(jax.random.fold_in(own, axis_at), (blocks,), jnp.float32, smallest / len(shards), high / len(shards)))
        gain = gain * jnp.repeat(steps, shape[axis_at] // blocks).reshape([-1 if axis == axis_at else 1 for axis in range(len(shape))])
    return gain


def noise(stream_key, shape, deviation, reach, pieces=(), held_as=jnp.bfloat16):
    level = block_levels(stream_key, shape, pieces, -0.22, 0.18) if pieces else 1.0
    values = jax.random.normal(stream_key, shape, jnp.float32) * deviation * level
    return jnp.minimum(jnp.maximum(values, -reach), reach).astype(held_as)


def setup_inputs(seed: int = 0) -> dict:
    key_of = jax.random.split(jax.random.key(seed), 6)
    return {
        "features": noise(key_of[0], (VERTICES, F), 1.0, 6.0, ((0, 1024),)),
        "tiles": noise(key_of[1], (N_ROW, N_COL, KMAX, TILE, TILE), (KMAX * TILE * TILE // (2 * MAST)) ** -0.5, 0.0546875, ((0, 64), (1, 16))),
        "places": draw_places(jax.random.fold_in(key_of[5], 71), 0),
        "counts": draw_counts(jax.random.fold_in(key_of[5], 71), 0),
        "weight": noise(key_of[4], (F, F), F ** -0.5, 0.375),
    }


def reference(features, tiles, places, counts, weight):
    tile_rows = N_ROW * MAST // TILE
    tile_cols = N_COL * MAST // TILE
    totals = jnp.zeros((N_COL, tile_rows * TILE, F), jnp.float32)

    def per_device(device, totals):
        row_index = (device // N_COL).astype(jnp.int32)
        col_index = (device % N_COL).astype(jnp.int32)

        def per_slot(slot_index, totals):
            position = places[row_index, col_index, slot_index].astype(jnp.int32)
            tile_row = position // tile_cols
            tile_col = position % tile_cols
            first = (row_index * (N_COL * MAST) + tile_col * TILE).astype(jnp.int32)
            source = lax.dynamic_slice(features, (first, jnp.int32(0)), (TILE, F))
            product = jnp.dot(tiles[row_index, col_index, slot_index], source, preferred_element_type=jnp.float32)
            begin = (col_index, (tile_row * TILE).astype(jnp.int32), jnp.int32(0))
            current = lax.dynamic_slice(totals, begin, (1, TILE, F))
            return lax.dynamic_update_slice(totals, current + product[None], begin)

        return lax.fori_loop(jnp.int32(0), counts[row_index, col_index].astype(jnp.int32), per_slot, totals)

    totals = lax.fori_loop(jnp.int32(0), jnp.int32(N_ROW * N_COL), per_device, totals)
    ordered = totals.reshape(N_COL, N_ROW, MAST, F).transpose(1, 0, 2, 3).reshape(N_ROW * N_COL * MAST, F)
    aggregated = ordered.astype(jnp.bfloat16)
    return jax.nn.relu(jnp.dot(aggregated, weight, preferred_element_type=jnp.float32)).astype(jnp.bfloat16)
```

```python
import functools

import jax
import jax.numpy as jnp
from jax import lax
from jax.experimental import pallas as pl
from jax.experimental.pallas import tpu as pltpu
from jax.sharding import PartitionSpec as P

MESH = pl.DeviceIdType.MESH
RING = 8
TILE = 128
MAST = 64
HALF = MAST // 2
SUBS = 4
F32 = jnp.float32
BF16 = jnp.bfloat16


def place_of(offset):
    far = offset // 4
    return far * (2 * offset - 8) + (1 - far) * (7 - 2 * offset)


def kernel(
    features, tiles, places, counts, weight, out,
    x_all, held, spots, limit, w_vmem, dense, part,
    send_far, recv_far, send_ring, recv_ring, send_last, recv_last, own,
    load_sem, gather_send, gather_recv, twin_send, twin_recv,
    far_send, far_recv, ring_send, ring_recv, last_send, last_recv,
):
    row = lax.axis_index("row")
    col = lax.axis_index("col")
    mz, mx = row // RING, row % RING
    my, core = col // 2, col % 2
    slots = tiles.shape[2]

    def around(axis, step):
        if axis == 0:
            return (((mz + step + RING) % RING) * RING + mx, col)
        if axis == 1:
            return (mz * RING + (mx + step + RING) % RING, col)
        return (row, ((my + step + RING) % RING) * 2 + core)

    twin = (row, my * 2 + 1 - core)

    loads = [
        pltpu.make_async_copy(features, x_all.at[col], load_sem.at[0]),
        pltpu.make_async_copy(places.at[0], spots, load_sem.at[1]),
        pltpu.make_async_copy(counts, limit, load_sem.at[2]),
        pltpu.make_async_copy(tiles.at[0, 0], held.at[pl.ds(0, slots)], load_sem.at[3]),
        pltpu.make_async_copy(weight, w_vmem, load_sem.at[4]),
    ]
    for load in loads:
        load.start()

    barrier = pltpu.get_barrier_semaphore()
    for axis in range(3):
        for step in range(1, RING):
            pl.semaphore_signal(barrier, inc=1, device_id=around(axis, step), device_id_type=MESH)
    pl.semaphore_signal(barrier, inc=1, device_id=twin, device_id_type=MESH)

    def remote(src, dst, send, recv, to):
        return pltpu.make_async_remote_copy(
            src_ref=src, dst_ref=dst, send_sem=send, recv_sem=recv, device_id=to, device_id_type=MESH
        )

    def gather_copy(step):
        mine = x_all.at[col]
        return remote(mine, mine, gather_send.at[step], gather_recv.at[step], around(2, step))

    def twin_copy(step):
        block = x_all.at[((my - step + RING) % RING) * 2 + core]
        return remote(block, block, twin_send.at[step], twin_recv.at[step], twin)

    loads[0].wait()
    pl.semaphore_wait(barrier, 3 * (RING - 1) + 1)
    for step in (4, 3, 5, 2, 6, 1, 7):
        gather_copy(step).start()
    twin_copy(0).start()

    held[slots] = jnp.zeros((TILE, TILE), BF16)
    for load in loads[1:]:
        load.wait()
    own_count = limit[0, 0]

    def fill(i, pointer):
        tz = i // 4
        oz = (tz - mz + RING) % RING
        qz = place_of(oz)
        for j in range(8):
            at = jnp.minimum(pointer, slots - 1)
            hit = jnp.where((spots[0, at] == i * 8 + j) & (pointer < own_count), 1, 0)
            slot = slots + hit * (pointer - slots)
            pointer = pointer + hit
            for side in range(2):
                ox = (2 * (i % 4) + side - mx + RING) % RING
                qx = place_of(ox)
                first = side * MAST
                lanes = pl.ds(j * TILE, TILE)
                dense[0, oz, qx, :, lanes] = held[slot, pl.ds(first, HALF), :]
                dense[1, ox, qz, :, lanes] = held[slot, pl.ds(first + HALF, HALF), :]
        return pointer

    lax.fori_loop(0, 32, fill, jnp.int32(0))

    for step in (1, 7, 2, 6, 3, 5, 4):
        gather_copy(step).wait_recv()
        twin_copy(step).start()
    for step in (0, 1, 7, 2, 6, 3, 5, 4):
        twin_copy(step).wait_recv()

    def compute(axis, offset):
        lhs = dense[axis, offset].reshape(RING * HALF, -1)
        rhs = x_all[...].reshape(-1, x_all.shape[-1])
        value = jnp.dot(lhs, rhs, preferred_element_type=F32)
        part[axis, offset] = value.reshape(part.shape[2:])

    def far_copy(d, u):
        return remote(
            send_far.at[d, u], recv_far.at[d, u], far_send.at[d, u], far_recv.at[d, u],
            around(d // 2, 2 - 4 * (d % 2)),
        )

    def ring_copy(d, step, sub):
        return remote(
            send_ring.at[d, step, sub], recv_ring.at[d, step, sub],
            ring_send.at[d, step, sub], ring_recv.at[d, step, sub],
            around(d // 2, 1 - 2 * (d % 2)),
        )

    def last_copy(axis, offset):
        return remote(
            send_last.at[axis, offset], recv_last.at[axis, offset],
            last_send.at[axis, offset], last_recv.at[axis, offset], around(1 - axis, offset),
        )

    def toward(d, steps):
        return steps if d % 2 == 0 else RING - steps

    for axis in range(2):
        compute(axis, 4)
        for d in (2 * axis, 2 * axis + 1):
            for u in range(2):
                send_far[d, u] = part[axis, 4, u + 2 * (d % 2)].astype(BF16)
                far_copy(d, u).start()
    for d in range(4):
        offset = toward(d, 3)
        compute(d // 2, offset)
        for sub in range(SUBS):
            send_ring[d, 0, sub] = part[d // 2, offset, sub].astype(BF16)
            ring_copy(d, 0, sub).start()

    for step in (1, 2):
        for d in range(4):
            compute(d // 2, toward(d, 3 - step))
        for sub in range(SUBS):
            for d in range(4):
                value = part[d // 2, toward(d, 3 - step), sub]
                if step == 1 and sub // 2 == d % 2:
                    far_copy(d, sub % 2).wait_recv()
                    value = value + recv_far[d, sub % 2].astype(F32)
                ring_copy(d, step - 1, sub).wait_recv()
                value = value + recv_ring[d, step - 1, sub].astype(F32)
                send_ring[d, step, sub] = value.astype(BF16)
                ring_copy(d, step, sub).start()

    for axis in range(2):
        compute(axis, 0)
    for sub in range(SUBS):
        for axis in range(2):
            value = part[axis, 0, sub]
            for d in (2 * axis, 2 * axis + 1):
                ring_copy(d, 2, sub).wait_recv()
                value = value + recv_ring[d, 2, sub].astype(F32)
            send_last[axis, 4 + sub] = value[:HALF].astype(BF16)
            last_copy(axis, 4 + sub).start()
            if sub < SUBS - 1:
                send_last[axis, 3 - sub] = value[HALF:].astype(BF16)
                last_copy(axis, 3 - sub).start()
            else:
                own[axis] = value[HALF:]

    for axis in range(2):
        total = own[axis]
        for offset in (4, 3, 5, 2, 6, 1, 7):
            last_copy(axis, offset).wait_recv()
            total = total + recv_last[axis, offset].astype(F32)
        own[axis] = total
    aggregated = own[...].reshape(MAST, -1).astype(BF16)
    hidden = jnp.dot(aggregated, w_vmem[...], preferred_element_type=F32)
    out[...] = jnp.maximum(hidden, 0.0).astype(BF16)

    for step in range(1, RING):
        gather_copy(step).wait_send()
    for step in range(RING):
        twin_copy(step).wait_send()
    for d in range(4):
        for u in range(2):
            far_copy(d, u).wait_send()
        for step in range(3):
            for sub in range(SUBS):
                ring_copy(d, step, sub).wait_send()
    for axis in range(2):
        for offset in range(1, RING):
            last_copy(axis, offset).wait_send()


def per_device(features, tiles, places, counts, weight):
    width = features.shape[1]
    slots = tiles.shape[2]
    piece = (2 * HALF, width)
    dma = pltpu.SemaphoreType.DMA
    anywhere = pl.BlockSpec(memory_space=pltpu.HBM)
    return pl.pallas_call(
        kernel,
        out_shape=jax.ShapeDtypeStruct(features.shape, BF16),
        in_specs=[anywhere] * 5,
        out_specs=pl.BlockSpec(memory_space=pltpu.VMEM),
        scratch_shapes=[
            pltpu.VMEM((2 * RING, MAST, width), BF16),
            pltpu.VMEM((slots + 1, TILE, TILE), BF16),
            pltpu.SMEM((1, slots), jnp.int32),
            pltpu.SMEM((1, 1), jnp.int32),
            pltpu.VMEM(weight.shape, BF16),
            pltpu.VMEM((2, RING, RING, HALF, RING * TILE), BF16),
            pltpu.VMEM((2, RING, SUBS) + piece, F32),
            pltpu.VMEM((4, 2) + piece, BF16),
            pltpu.VMEM((4, 2) + piece, BF16),
            pltpu.VMEM((4, 3, SUBS) + piece, BF16),
            pltpu.VMEM((4, 3, SUBS) + piece, BF16),
            pltpu.VMEM((2, RING, HALF, width), BF16),
            pltpu.VMEM((2, RING, HALF, width), BF16),
            pltpu.VMEM((2, HALF, width), F32),
            dma((5,)),
            dma((RING,)),
            dma((RING,)),
            dma((RING,)),
            dma((RING,)),
            dma((4, 2)),
            dma((4, 2)),
            dma((4, 3, SUBS)),
            dma((4, 3, SUBS)),
            dma((2, RING)),
            dma((2, RING)),
        ],
        compiler_params=pltpu.CompilerParams(
            collective_id=0, has_side_effects=True, vmem_limit_bytes=60 * 2**20
        ),
    )(features, tiles, places, counts, weight)


def solution(mesh):
    return jax.shard_map(
        per_device,
        mesh=mesh,
        in_specs=(
            P(("row", "col"), None),
            P("row", "col", None, None, None),
            P("row", "col", None),
            P("row", "col"),
            P(),
        ),
        out_specs=P(("row", "col"), None),
        check_vma=False,
    )
```

```python
import functools

import jax
import jax.numpy as jnp
from jax import lax
from jax.experimental import pallas as pl
from jax.experimental.pallas import tpu as pltpu
from jax.sharding import PartitionSpec as P

MESH = pl.DeviceIdType.MESH
RING = 8
TILE = 128
MAST = 64
HALF = MAST // 2
SIDES = 2
SUB = RING * HALF // 2
FAR_FIRST = (4, 3, 5, 2, 6, 1, 7)
NEAR_FIRST = (1, 7, 2, 6, 3, 5, 4)
ORDER = (4, 3, 5, 2, 6, 1, 7, 0)
F32 = jnp.float32
BF16 = jnp.bfloat16


def place_of(offset):
    far = offset // 4
    return far * (2 * offset - 8) + (1 - far) * (7 - 2 * offset)


def kernel(
    features, tiles, places, counts, weight, out,
    x_all, held, spots, limit, w_vmem, dense, part,
    send_far, recv_far, send_ring, recv_ring, send_last, recv_last, own,
    load_sem, gather_send, gather_recv, pair_send, pair_recv, twin_send, twin_recv,
    far_send, far_recv, ring_send, ring_recv, last_send, last_recv,
):
    row = lax.axis_index("row")
    col = lax.axis_index("col")
    mz, mx = row // RING, row % RING
    my, core = col // 2, col % 2
    slots = tiles.shape[2]
    lanes = features.shape[1] // SIDES

    def around(axis, step):
        if axis == 0:
            return (((mz + step + RING) % RING) * RING + mx, col)
        return (mz * RING + (mx + step + RING) % RING, col)

    def along(step, which):
        return (row, ((my + step + RING) % RING) * 2 + which)

    twin = (row, my * 2 + 1 - core)

    loads = [
        pltpu.make_async_copy(features.at[:, pl.ds(h * lanes, lanes)], x_all.at[h, col], load_sem.at[h])
        for h in range(SIDES)
    ]
    loads += [
        pltpu.make_async_copy(tiles.at[0, 0], held.at[pl.ds(0, slots)], load_sem.at[2]),
        pltpu.make_async_copy(places.at[0], spots, load_sem.at[3]),
        pltpu.make_async_copy(counts, limit, load_sem.at[4]),
        pltpu.make_async_copy(weight, w_vmem, load_sem.at[5]),
    ]
    for load in loads:
        load.start()

    barrier = pltpu.get_barrier_semaphore()

    def greet(to):
        pl.semaphore_signal(barrier, inc=1, device_id=to, device_id_type=MESH)

    @pl.when(core == 1)
    def _():
        for step in FAR_FIRST:
            greet(along(step, 0))
            greet(along(step, 1))

    for axis in range(2):
        for step in (2, 6, 1, 7):
            greet(around(axis, step))
    greet(twin)

    def remote(src, dst, send, recv, to):
        return pltpu.make_async_remote_copy(
            src_ref=src, dst_ref=dst, send_sem=send, recv_sem=recv, device_id=to, device_id_type=MESH
        )

    def gather_copy(h, step):
        mine = x_all.at[h, col]
        return remote(mine, mine, gather_send.at[h, step], gather_recv.at[h, core, step], along(step, 1))

    def arrival(h, which, step):
        block = x_all.at[h, ((my - step + RING) % RING) * 2 + which]
        return remote(block, block, gather_send.at[h, step], gather_recv.at[h, which, step], twin)

    def pair_copy(h, step):
        pair = x_all.at[h, pl.ds(((my - step + RING) % RING) * 2, 2)]
        return remote(pair, pair, pair_send.at[h, step], pair_recv.at[h, step], twin)

    def twin_copy(h):
        mine = x_all.at[h, col]
        return remote(mine, mine, twin_send.at[h], twin_recv.at[h], twin)

    for h in range(SIDES):
        loads[h].wait()
    pl.semaphore_wait(barrier, 16)
    for h in range(SIDES):
        for step in FAR_FIRST:
            gather_copy(h, step).start()
        twin_copy(h).start()

    held[slots] = jnp.zeros((TILE, TILE), BF16)
    for load in loads[SIDES:]:
        load.wait()
    own_count = limit[0, 0]

    def fill(i, pointer):
        oz = (i // 4 - mz + RING) % RING
        qz = place_of(oz)
        for j in range(8):
            at = jnp.minimum(pointer, slots - 1)
            hit = jnp.where((spots[0, at] == i * 8 + j) & (pointer < own_count), 1, 0)
            slot = slots + hit * (pointer - slots)
            pointer = pointer + hit
            for side in range(2):
                ox = (2 * (i % 4) + side - mx + RING) % RING
                qx = place_of(ox)
                first = side * MAST
                columns = pl.ds(j * TILE, TILE)
                dense[0, oz, qx, :, columns] = held[slot, pl.ds(first, HALF), :]
                dense[1, ox, qz, :, columns] = held[slot, pl.ds(first + HALF, HALF), :]
        return pointer

    lax.fori_loop(0, 32, fill, jnp.int32(0))

    def collect(h):
        @pl.when(core == 1)
        def _():
            for step in NEAR_FIRST:
                for which in range(2):
                    arrival(h, which, step).wait_recv()
                pair_copy(h, step).start()

        @pl.when(core == 0)
        def _():
            for step in NEAR_FIRST:
                pair_copy(h, step).wait_recv()

        twin_copy(h).wait_recv()

    def product(axis, offset, rhs):
        lhs = dense[axis, offset].reshape(RING * HALF, -1)
        return jnp.dot(lhs, rhs, preferred_element_type=F32)

    def source(h):
        return x_all[h].reshape(-1, lanes)

    def far_copy(d, h):
        return remote(
            send_far.at[d, h], recv_far.at[d, h], far_send.at[d, h], far_recv.at[d, h],
            around(d // 2, 2 - 4 * (d % 2)),
        )

    def ring_copy(d, step, h, sub):
        return remote(
            send_ring.at[d, step, h, sub], recv_ring.at[d, step, h, sub],
            ring_send.at[d, step, h, sub], ring_recv.at[d, step, h, sub],
            around(d // 2, 1 - 2 * (d % 2)),
        )

    def last_copy(axis, offset, h):
        return remote(
            send_last.at[axis, offset, h], recv_last.at[axis, offset, h],
            last_send.at[axis, offset, h], last_recv.at[axis, offset, h], around(1 - axis, offset),
        )

    def toward(d, steps):
        return steps if d % 2 == 0 else RING - steps

    for h in range(SIDES):
        collect(h)
        for axis in range(2):
            value = product(axis, 4, source(h)).astype(BF16).reshape(2, SUB, lanes)
            for d in (2 * axis, 2 * axis + 1):
                send_far[d, h] = value[d % 2]
                far_copy(d, h).start()
        for d in range(4):
            value = product(d // 2, toward(d, 3), source(h)).astype(BF16).reshape(2, SUB, lanes)
            for sub in range(2):
                send_ring[d, 0, h, sub] = value[sub]
                ring_copy(d, 0, h, sub).start()

    def compute(axis, offset):
        rhs = jnp.concatenate([source(h) for h in range(SIDES)], axis=1)
        value = product(axis, offset, rhs)
        for h in range(SIDES):
            part[axis, offset, h] = value[:, h * lanes : (h + 1) * lanes].reshape(2, SUB, lanes)

    for step in (1, 2):
        for d in range(4):
            compute(d // 2, toward(d, 3 - step))
        for h in range(SIDES):
            for sub in range(2):
                for d in range(4):
                    value = part[d // 2, toward(d, 3 - step), h, sub]
                    if step == 1 and sub == d % 2:
                        far_copy(d, h).wait_recv()
                        value = value + recv_far[d, h].astype(F32)
                    ring_copy(d, step - 1, h, sub).wait_recv()
                    value = value + recv_ring[d, step - 1, h, sub].astype(F32)
                    send_ring[d, step, h, sub] = value.astype(BF16)
                    ring_copy(d, step, h, sub).start()

    for axis in range(2):
        compute(axis, 0)
    for h in range(SIDES):
        for sub in range(2):
            for axis in range(2):
                value = part[axis, 0, h, sub]
                for d in (2 * axis, 2 * axis + 1):
                    ring_copy(d, 2, h, sub).wait_recv()
                    value = value + recv_ring[d, 2, h, sub].astype(F32)
                for t in range(4):
                    offset = ORDER[4 * sub + t]
                    piece = value[t * HALF : (t + 1) * HALF]
                    if offset:
                        send_last[axis, offset, h] = piece.astype(BF16)
                        last_copy(axis, offset, h).start()
                    else:
                        own[axis, h] = piece

    for h in range(SIDES):
        for axis in range(2):
            total = own[axis, h]
            for offset in FAR_FIRST:
                last_copy(axis, offset, h).wait_recv()
                total = total + recv_last[axis, offset, h].astype(F32)
            own[axis, h] = total
    aggregated = jnp.concatenate([own[:, h].reshape(MAST, lanes) for h in range(SIDES)], axis=1).astype(BF16)
    hidden = jnp.dot(aggregated, w_vmem[...], preferred_element_type=F32)
    out[...] = jnp.maximum(hidden, 0.0).astype(BF16)

    for h in range(SIDES):
        twin_copy(h).wait_send()
        for step in range(1, RING):
            gather_copy(h, step).wait_send()
        for d in range(4):
            far_copy(d, h).wait_send()
            for step in range(3):
                for sub in range(2):
                    ring_copy(d, step, h, sub).wait_send()
        for axis in range(2):
            for offset in range(1, RING):
                last_copy(axis, offset, h).wait_send()

    @pl.when(core == 1)
    def _():
        for h in range(SIDES):
            for step in range(1, RING):
                pair_copy(h, step).wait_send()


def per_device(features, tiles, places, counts, weight):
    width = features.shape[1]
    slots = tiles.shape[2]
    lanes = width // SIDES
    piece = (SUB, lanes)
    dma = pltpu.SemaphoreType.DMA
    anywhere = pl.BlockSpec(memory_space=pltpu.HBM)
    return pl.pallas_call(
        kernel,
        out_shape=jax.ShapeDtypeStruct(features.shape, BF16),
        in_specs=[anywhere] * 5,
        out_specs=pl.BlockSpec(memory_space=pltpu.VMEM),
        scratch_shapes=[
            pltpu.VMEM((SIDES, 2 * RING, MAST, lanes), BF16),
            pltpu.VMEM((slots + 1, TILE, TILE), BF16),
            pltpu.SMEM((1, slots), jnp.int32),
            pltpu.SMEM((1, 1), jnp.int32),
            pltpu.VMEM(weight.shape, BF16),
            pltpu.VMEM((2, RING, RING, HALF, RING * TILE), BF16),
            pltpu.VMEM((2, RING, SIDES, 2) + piece, F32),
            pltpu.VMEM((4, SIDES) + piece, BF16),
            pltpu.VMEM((4, SIDES) + piece, BF16),
            pltpu.VMEM((4, 3, SIDES, 2) + piece, BF16),
            pltpu.VMEM((4, 3, SIDES, 2) + piece, BF16),
            pltpu.VMEM((2, RING, SIDES, HALF, lanes), BF16),
            pltpu.VMEM((2, RING, SIDES, HALF, lanes), BF16),
            pltpu.VMEM((2, SIDES, HALF, lanes), F32),
            dma((6,)),
            dma((SIDES, RING)),
            dma((SIDES, 2, RING)),
            dma((SIDES, RING)),
            dma((SIDES, RING)),
            dma((SIDES,)),
            dma((SIDES,)),
            dma((4, SIDES)),
            dma((4, SIDES)),
            dma((4, 3, SIDES, 2)),
            dma((4, 3, SIDES, 2)),
            dma((2, RING, SIDES)),
            dma((2, RING, SIDES)),
        ],
        compiler_params=pltpu.CompilerParams(
            collective_id=0, has_side_effects=True, vmem_limit_bytes=60 * 2**20
        ),
    )(features, tiles, places, counts, weight)


def solution(mesh):
    return jax.shard_map(
        per_device,
        mesh=mesh,
        in_specs=(
            P(("row", "col"), None),
            P("row", "col", None, None, None),
            P("row", "col", None),
            P("row", "col"),
            P(),
        ),
        out_specs=P(("row", "col"), None),
        check_vma=False,
    )
```

```python
import functools

import jax
import jax.numpy as jnp
from jax import lax
from jax.experimental import pallas as pl
from jax.experimental.pallas import tpu as pltpu
from jax.sharding import PartitionSpec as P

MESH = pl.DeviceIdType.MESH
RING = 8
TILE = 128
MAST = 64
HALF = MAST // 2
SIDES = 2
SUBS = 2
SUB = RING * HALF // SUBS
FAR_FIRST = (4, 3, 5, 2, 6, 1, 7)
NEAR_FIRST = (1, 7, 2, 6, 3, 5, 4)
ORDER = (4, 3, 5, 2, 6, 1, 7, 0)
F32 = jnp.float32
BF16 = jnp.bfloat16


def place_of(offset):
    far = offset // 4
    return far * (2 * offset - 8) + (1 - far) * (7 - 2 * offset)


def kernel(
    features, tiles, places, counts, weight, out,
    x_all, held, spots, limit, w_vmem, dense, part,
    send_far, recv_far, send_ring, recv_ring, send_last, recv_last, own,
    load_sem, gather_send, gather_recv, pair_send, pair_recv, twin_send, twin_recv,
    far_send, far_recv, ring_send, ring_recv, last_send, last_recv,
):
    row = lax.axis_index("row")
    col = lax.axis_index("col")
    mz, mx = row // RING, row % RING
    my, core = col // 2, col % 2
    slots = tiles.shape[2]
    lanes = features.shape[1] // SIDES

    def around(axis, step):
        if axis == 0:
            return (((mz + step + RING) % RING) * RING + mx, col)
        return (mz * RING + (mx + step + RING) % RING, col)

    def along(step, which):
        return (row, ((my + step + RING) % RING) * 2 + which)

    twin = (row, my * 2 + 1 - core)

    def half(h):
        return features.at[:, pl.ds(h * lanes, lanes)]

    loads = [pltpu.make_async_copy(half(h), x_all.at[h, col], load_sem.at[h]) for h in range(SIDES)]
    loads += [
        pltpu.make_async_copy(tiles.at[0, 0], held.at[pl.ds(0, slots)], load_sem.at[2]),
        pltpu.make_async_copy(places.at[0], spots, load_sem.at[3]),
        pltpu.make_async_copy(counts, limit, load_sem.at[4]),
        pltpu.make_async_copy(weight, w_vmem, load_sem.at[5]),
    ]
    barrier = pltpu.get_barrier_semaphore()

    def greet(to):
        pl.semaphore_signal(barrier, inc=1, device_id=to, device_id_type=MESH)

    @pl.when(core == 1)
    def _():
        for step in FAR_FIRST:
            greet(along(step, 0))
            greet(along(step, 1))

    for axis in range(2):
        for step in (2, 6, 1, 7):
            greet(around(axis, step))
    greet(twin)

    def remote(src, dst, send, recv, to):
        return pltpu.make_async_remote_copy(
            src_ref=src, dst_ref=dst, send_sem=send, recv_sem=recv, device_id=to, device_id_type=MESH
        )

    def gather_copy(h, step):
        return remote(
            x_all.at[h, col], x_all.at[h, col], gather_send.at[0], gather_recv.at[h, step], along(step, 1)
        )

    def pair_of(h, step):
        return x_all.at[h, pl.ds(((my - step + RING) % RING) * 2, 2)]

    def arrival(h, step):
        return remote(pair_of(h, step), pair_of(h, step), gather_send.at[0], gather_recv.at[h, step], twin)

    def pair_copy(h, step):
        return remote(pair_of(h, step), pair_of(h, step), pair_send.at[0], pair_recv.at[h], twin)

    def all_of(ref, send, recv):
        return remote(ref, ref, send, recv, twin)

    def twin_copy(h):
        return remote(x_all.at[h, col], x_all.at[h, col], twin_send.at[h], twin_recv.at[h], twin)

    for load in loads:
        load.start()
    for h in range(SIDES):
        loads[h].wait()
    pl.semaphore_wait(barrier, 16)
    for h in range(SIDES):
        for step in FAR_FIRST:
            gather_copy(h, step).start()
        twin_copy(h).start()

    held[slots] = jnp.zeros((TILE, TILE), BF16)
    for load in loads[SIDES:]:
        load.wait()
    own_count = limit[0, 0]

    def fill(i, pointer):
        oz = (i // 4 - mz + RING) % RING
        qz = place_of(oz)
        for j in range(8):
            at = jnp.minimum(pointer, slots - 1)
            hit = jnp.where((spots[0, at] == i * 8 + j) & (pointer < own_count), 1, 0)
            slot = slots + hit * (pointer - slots)
            pointer = pointer + hit
            for side in range(2):
                ox = (2 * (i % 4) + side - mx + RING) % RING
                qx = place_of(ox)
                first = side * MAST
                columns = pl.ds(j * TILE, TILE)
                dense[0, oz, qx, :, columns] = held[slot, pl.ds(first, HALF), :]
                dense[1, ox, qz, :, columns] = held[slot, pl.ds(first + HALF, HALF), :]
        return pointer

    lax.fori_loop(0, 32, fill, jnp.int32(0))

    def collect(h):
        @pl.when(core == 1)
        def _():
            for step in NEAR_FIRST:
                arrival(h, step).wait_recv()
                pair_copy(h, step).start()

        @pl.when(core == 0)
        def _():
            pairs = x_all.at[h, pl.ds(0, 2 * (RING - 1))]
            all_of(pairs, pair_send.at[0], pair_recv.at[h]).wait_recv()

        twin_copy(h).wait_recv()

    def product(axis, offset, rhs):
        lhs = dense[axis, offset].reshape(RING * HALF, -1)
        return jnp.dot(lhs, rhs, preferred_element_type=F32)

    def source(h):
        return x_all[h].reshape(-1, lanes)

    def far_copy(d, h, u):
        return remote(
            send_far.at[d, h, u], recv_far.at[d, h, u], far_send.at[0], far_recv.at[d, h, u],
            around(d // 2, 2 - 4 * (d % 2)),
        )

    def ring_copy(d, slot, h, sub):
        return remote(
            send_ring.at[d, slot, h, sub], recv_ring.at[d, slot, h, sub],
            ring_send.at[0], ring_recv.at[d, slot, h, sub],
            around(d // 2, 1 - 2 * (d % 2)),
        )

    def last_copy(axis, offset, h):
        return remote(
            send_last.at[h, axis, offset], recv_last.at[h, axis, offset],
            last_send.at[0], last_recv.at[h], around(1 - axis, offset),
        )

    def toward(d, steps):
        return steps if d % 2 == 0 else RING - steps

    def products(h, offsets):
        values = [product(axis, offset, source(h)) for axis, offset in offsets]
        return [value.reshape(SUBS, SUB, lanes) for value in values]

    def keep(offsets):
        rhs = jnp.concatenate([source(h) for h in range(SIDES)], axis=1)
        for axis, offset in offsets:
            value = product(axis, offset, rhs)
            for h in range(SIDES):
                part[axis, offset, h] = value[:, h * lanes : (h + 1) * lanes].reshape(SUBS, SUB, lanes)

    def at_distance(steps):
        return [(d // 2, toward(d, steps)) for d in range(4)]

    def send_farthest(h):
        values = products(h, [(0, 4), (1, 4)])
        for d in range(4):
            for u in range(SUBS // 2):
                send_far[d, h, u] = values[d // 2][SUBS // 2 * (d % 2) + u].astype(BF16)
        for u in range(SUBS // 2):
            for d in range(4):
                far_copy(d, h, u).start()

    def send_fresh(h, steps, slot):
        values = products(h, at_distance(steps))
        for d in range(4):
            send_ring[d, slot, h] = values[d].astype(BF16)
        for sub in range(SUBS):
            for d in range(4):
                ring_copy(d, slot, h, sub).start()

    def pass_on(h, steps, slot):
        for sub in range(SUBS):
            for d in range(4):
                value = part[d // 2, toward(d, steps), h, sub]
                u = sub - SUBS // 2 * (d % 2)
                if slot == 0 and 0 <= u < SUBS // 2:
                    far_copy(d, h, u).wait_recv()
                    value = value + recv_far[d, h, u].astype(F32)
                ring_copy(d, slot, h, sub).wait_recv()
                value = value + recv_ring[d, slot, h, sub].astype(F32)
                send_ring[d, slot + 1, h, sub] = value.astype(BF16)
                ring_copy(d, slot + 1, h, sub).start()

    for h in range(SIDES):
        collect(h)
        send_farthest(h)
        send_fresh(h, 3, 0)
    keep(at_distance(2))
    pass_on(0, 2, 0)
    keep(at_distance(1))
    keep([(0, 0), (1, 0)])
    pass_on(1, 2, 0)
    for h in range(SIDES):
        pass_on(h, 1, 1)

    for h in range(SIDES):
        for sub in range(SUBS):
            for axis in range(2):
                value = part[axis, 0, h, sub]
                for d in (2 * axis, 2 * axis + 1):
                    ring_copy(d, 2, h, sub).wait_recv()
                    value = value + recv_ring[d, 2, h, sub].astype(F32)
                for t in range(SUB // HALF):
                    offset = ORDER[SUB // HALF * sub + t]
                    piece = value[t * HALF : (t + 1) * HALF]
                    if offset:
                        send_last[h, axis, offset] = piece.astype(BF16)
                        last_copy(axis, offset, h).start()
                    else:
                        own[axis, h] = piece

    for h in range(SIDES):
        all_of(recv_last.at[h, :, pl.ds(1, RING - 1)], last_send.at[0], last_recv.at[h]).wait_recv()
        for axis in range(2):
            total = own[axis, h]
            for offset in FAR_FIRST:
                total = total + recv_last[h, axis, offset].astype(F32)
            own[axis, h] = total
    aggregated = jnp.concatenate([own[:, h].reshape(MAST, lanes) for h in range(SIDES)], axis=1).astype(BF16)
    hidden = jnp.dot(aggregated, w_vmem[...], preferred_element_type=F32)
    out[...] = jnp.maximum(hidden, 0.0).astype(BF16)

    for h in range(SIDES):
        twin_copy(h).wait_send()
    all_of(x_all.at[:, pl.ds(0, RING - 1)], gather_send.at[0], gather_recv.at[0, 0]).wait_send()
    all_of(send_last.at[:, :, pl.ds(1, RING - 1)], last_send.at[0], last_recv.at[0]).wait_send()
    all_of(send_far, far_send.at[0], far_recv.at[0, 0, 0]).wait_send()
    all_of(send_ring, ring_send.at[0], ring_recv.at[0, 0, 0, 0]).wait_send()

    @pl.when(core == 1)
    def _():
        pairs = x_all.at[:, pl.ds(0, 2 * (RING - 1))]
        all_of(pairs, pair_send.at[0], pair_recv.at[0]).wait_send()


def per_device(features, tiles, places, counts, weight):
    width = features.shape[1]
    slots = tiles.shape[2]
    lanes = width // SIDES
    piece = (SUB, lanes)
    dma = pltpu.SemaphoreType.DMA
    anywhere = pl.BlockSpec(memory_space=pltpu.HBM)
    return pl.pallas_call(
        kernel,
        out_shape=jax.ShapeDtypeStruct(features.shape, BF16),
        in_specs=[anywhere] * 5,
        out_specs=pl.BlockSpec(memory_space=pltpu.VMEM),
        scratch_shapes=[
            pltpu.VMEM((SIDES, 2 * RING, MAST, lanes), BF16),
            pltpu.VMEM((slots + 1, TILE, TILE), BF16),
            pltpu.SMEM((1, slots), jnp.int32),
            pltpu.SMEM((1, 1), jnp.int32),
            pltpu.VMEM(weight.shape, BF16),
            pltpu.VMEM((2, RING, RING, HALF, RING * TILE), BF16),
            pltpu.VMEM((2, RING, SIDES, SUBS) + piece, F32),
            pltpu.VMEM((4, SIDES, SUBS // 2) + piece, BF16),
            pltpu.VMEM((4, SIDES, SUBS // 2) + piece, BF16),
            pltpu.VMEM((4, 3, SIDES, SUBS) + piece, BF16),
            pltpu.VMEM((4, 3, SIDES, SUBS) + piece, BF16),
            pltpu.VMEM((SIDES, 2, RING, HALF, lanes), BF16),
            pltpu.VMEM((SIDES, 2, RING, HALF, lanes), BF16),
            pltpu.VMEM((2, SIDES, HALF, lanes), F32),
            dma((6,)),
            dma((1,)),
            dma((SIDES, RING)),
            dma((1,)),
            dma((SIDES,)),
            dma((SIDES,)),
            dma((SIDES,)),
            dma((1,)),
            dma((4, SIDES, SUBS // 2)),
            dma((1,)),
            dma((4, 3, SIDES, SUBS)),
            dma((1,)),
            dma((SIDES,)),
        ],
        compiler_params=pltpu.CompilerParams(
            collective_id=0, has_side_effects=True, vmem_limit_bytes=55168 * 2**10
        ),
    )(features, tiles, places, counts, weight)


def solution(mesh):
    return jax.shard_map(
        per_device,
        mesh=mesh,
        in_specs=(
            P(("row", "col"), None),
            P("row", "col", None, None, None),
            P("row", "col", None),
            P("row", "col"),
            P(),
        ),
        out_specs=P(("row", "col"), None),
        check_vma=False,
    )
```

```python
import functools

import jax
import jax.numpy as jnp
from jax import lax
from jax.experimental import pallas as pl
from jax.experimental.pallas import tpu as pltpu
from jax.sharding import PartitionSpec as P

MESH = pl.DeviceIdType.MESH
RING = 8
TILE = 128
MAST = 64
HALF = MAST // 2
SIDES = 2
SUBS = 2
SUB = RING * HALF // SUBS
FAR_FIRST = (4, 3, 5, 2, 6, 1, 7)
NEAR_FIRST = (1, 7, 2, 6, 3, 5, 4)
ORDER = (4, 3, 5, 2, 6, 1, 7, 0)
F32 = jnp.float32
BF16 = jnp.bfloat16


def place_of(offset):
    far = offset // 4
    return far * (2 * offset - 8) + (1 - far) * (7 - 2 * offset)


def kernel(
    features, tiles, places, counts, weight, out,
    x_all, held, spots, limit, w_vmem, dense, part,
    send_far, recv_far, send_ring, recv_ring, send_last, recv_last, own,
    load_sem, gather_send, gather_recv, pair_send, pair_recv, twin_send, twin_recv,
    far_send, ring_send, ring_recv, last_send, last_recv,
):
    row = lax.axis_index("row")
    col = lax.axis_index("col")
    mz, mx = row // RING, row % RING
    my, core = col // 2, col % 2
    slots = tiles.shape[2]
    lanes = features.shape[1] // SIDES

    def around(axis, step):
        if axis == 0:
            return (((mz + step + RING) % RING) * RING + mx, col)
        return (mz * RING + (mx + step + RING) % RING, col)

    def along(step, which):
        return (row, ((my + step + RING) % RING) * 2 + which)

    twin = (row, my * 2 + 1 - core)

    def half(h):
        return features.at[:, pl.ds(h * lanes, lanes)]

    loads = [pltpu.make_async_copy(half(h), x_all.at[h, col], load_sem.at[h]) for h in range(SIDES)]
    loads += [
        pltpu.make_async_copy(tiles.at[0, 0], held.at[pl.ds(0, slots)], load_sem.at[2]),
        pltpu.make_async_copy(places.at[0], spots, load_sem.at[3]),
        pltpu.make_async_copy(counts, limit, load_sem.at[4]),
        pltpu.make_async_copy(weight, w_vmem, load_sem.at[5]),
    ]
    barrier = pltpu.get_barrier_semaphore()

    def greet(to):
        pl.semaphore_signal(barrier, inc=1, device_id=to, device_id_type=MESH)

    @pl.when(core == 1)
    def _():
        for step in FAR_FIRST:
            greet(along(step, 0))
            greet(along(step, 1))

    for axis in range(2):
        for step in (2, 6, 1, 7):
            greet(around(axis, step))
    greet(twin)

    def remote(src, dst, send, recv, to):
        return pltpu.make_async_remote_copy(
            src_ref=src, dst_ref=dst, send_sem=send, recv_sem=recv, device_id=to, device_id_type=MESH
        )

    def gather_copy(h, step):
        return remote(
            x_all.at[h, col], x_all.at[h, col], gather_send.at[0], gather_recv.at[h, step], along(step, 1)
        )

    def pair_of(h, step):
        return x_all.at[h, pl.ds(((my - step + RING) % RING) * 2, 2)]

    def arrival(h, step):
        return remote(pair_of(h, step), pair_of(h, step), gather_send.at[0], gather_recv.at[h, step], twin)

    def pair_copy(h, step):
        return remote(pair_of(h, step), pair_of(h, step), pair_send.at[0], pair_recv.at[h], twin)

    def all_of(ref, send, recv):
        return remote(ref, ref, send, recv, twin)

    def twin_copy(h):
        return remote(x_all.at[h, col], x_all.at[h, col], twin_send.at[h], twin_recv.at[h], twin)

    for load in loads:
        load.start()
    for h in range(SIDES):
        loads[h].wait()
    pl.semaphore_wait(barrier, 16)
    for h in range(SIDES):
        for step in FAR_FIRST:
            gather_copy(h, step).start()
        twin_copy(h).start()

    held[slots] = jnp.zeros((TILE, TILE), BF16)
    for load in loads[SIDES:]:
        load.wait()
    own_count = limit[0, 0]

    def fill(i, pointer):
        oz = (i // 4 - mz + RING) % RING
        qz = place_of(oz)
        for j in range(8):
            at = jnp.minimum(pointer, slots - 1)
            hit = jnp.where((spots[0, at] == i * 8 + j) & (pointer < own_count), 1, 0)
            slot = slots + hit * (pointer - slots)
            pointer = pointer + hit
            for side in range(2):
                ox = (2 * (i % 4) + side - mx + RING) % RING
                qx = place_of(ox)
                first = side * MAST
                columns = pl.ds(j * TILE, TILE)
                dense[0, oz, qx, :, columns] = held[slot, pl.ds(first, HALF), :]
                dense[1, ox, qz, :, columns] = held[slot, pl.ds(first + HALF, HALF), :]
        return pointer

    lax.fori_loop(0, 32, fill, jnp.int32(0))

    def collect(h):
        @pl.when(core == 1)
        def _():
            for step in NEAR_FIRST:
                arrival(h, step).wait_recv()
                pair_copy(h, step).start()

        @pl.when(core == 0)
        def _():
            pairs = x_all.at[h, pl.ds(0, 2 * (RING - 1))]
            all_of(pairs, pair_send.at[0], pair_recv.at[h]).wait_recv()

        twin_copy(h).wait_recv()

    def product(axis, offset, rhs):
        lhs = dense[axis, offset].reshape(RING * HALF, -1)
        return jnp.dot(lhs, rhs, preferred_element_type=F32)

    def source(h):
        return x_all[h].reshape(-1, lanes)

    def far_copy(d, h, u):
        return remote(
            send_far.at[d, h, u], recv_far.at[d, h, u], far_send.at[0], ring_recv.at[d, 0, h, SUBS // 2 * (d % 2) + u],
            around(d // 2, 2 - 4 * (d % 2)),
        )

    def ring_copy(d, slot, h, sub):
        return remote(
            send_ring.at[d, slot, h, sub], recv_ring.at[d, slot, h, sub],
            ring_send.at[0], ring_recv.at[d if slot < 2 else d - d % 2, slot, h, sub],
            around(d // 2, 1 - 2 * (d % 2)),
        )

    def two_pieces(d, slot, h, sub):
        return all_of(recv_ring.at[d, slot, h, pl.ds(0, 2)], ring_send.at[0], ring_recv.at[d, slot, h, sub])

    def last_copy(axis, offset, h):
        return remote(
            send_last.at[h, axis, offset], recv_last.at[h, axis, offset],
            last_send.at[0], last_recv.at[h], around(1 - axis, offset),
        )

    def toward(d, steps):
        return steps if d % 2 == 0 else RING - steps

    def products(h, offsets):
        values = [product(axis, offset, source(h)) for axis, offset in offsets]
        return [value.reshape(SUBS, SUB, lanes) for value in values]

    def keep(offsets):
        rhs = jnp.concatenate([source(h) for h in range(SIDES)], axis=1)
        for axis, offset in offsets:
            value = product(axis, offset, rhs)
            for h in range(SIDES):
                part[axis, offset, h] = value[:, h * lanes : (h + 1) * lanes].reshape(SUBS, SUB, lanes)

    def at_distance(steps):
        return [(d // 2, toward(d, steps)) for d in range(4)]

    def send_farthest(h):
        values = products(h, [(0, 4), (1, 4)])
        for d in range(4):
            for u in range(SUBS // 2):
                send_far[d, h, u] = values[d // 2][SUBS // 2 * (d % 2) + u].astype(BF16)
        for u in range(SUBS // 2):
            for d in range(4):
                far_copy(d, h, u).start()

    def send_fresh(h, steps, slot):
        values = products(h, at_distance(steps))
        for d in range(4):
            send_ring[d, slot, h] = values[d].astype(BF16)
        for sub in range(SUBS):
            for d in range(4):
                ring_copy(d, slot, h, sub).start()

    def pass_on(h, steps, slot):
        for sub in range(SUBS):
            for d in range(4):
                value = part[d // 2, toward(d, steps), h, sub]
                u = sub - SUBS // 2 * (d % 2)
                if slot == 0 and 0 <= u < SUBS // 2:
                    two_pieces(d, 0, h, sub).wait_recv()
                    value = value + recv_far[d, h, u].astype(F32)
                else:
                    ring_copy(d, slot, h, sub).wait_recv()
                value = value + recv_ring[d, slot, h, sub].astype(F32)
                send_ring[d, slot + 1, h, sub] = value.astype(BF16)
                ring_copy(d, slot + 1, h, sub).start()

    for h in range(SIDES):
        collect(h)
        send_farthest(h)
        send_fresh(h, 3, 0)
    keep(at_distance(2))
    pass_on(0, 2, 0)
    keep(at_distance(1))
    keep([(0, 0), (1, 0)])
    pass_on(1, 2, 0)
    for h in range(SIDES):
        pass_on(h, 1, 1)

    for h in range(SIDES):
        for sub in range(SUBS):
            for axis in range(2):
                value = part[axis, 0, h, sub]
                two_pieces(2 * axis, 2, h, sub).wait_recv()
                for d in (2 * axis, 2 * axis + 1):
                    value = value + recv_ring[d, 2, h, sub].astype(F32)
                for t in range(SUB // HALF):
                    offset = ORDER[SUB // HALF * sub + t]
                    piece = value[t * HALF : (t + 1) * HALF]
                    if offset:
                        send_last[h, axis, offset] = piece.astype(BF16)
                        last_copy(axis, offset, h).start()
                    else:
                        own[axis, h] = piece

    for h in range(SIDES):
        all_of(recv_last.at[h, :, pl.ds(1, RING - 1)], last_send.at[0], last_recv.at[h]).wait_recv()
        for axis in range(2):
            total = own[axis, h]
            for offset in FAR_FIRST:
                total = total + recv_last[h, axis, offset].astype(F32)
            own[axis, h] = total
    aggregated = jnp.concatenate([own[:, h].reshape(MAST, lanes) for h in range(SIDES)], axis=1).astype(BF16)
    hidden = jnp.dot(aggregated, w_vmem[...], preferred_element_type=F32)
    out[...] = jnp.maximum(hidden, 0.0).astype(BF16)

    for h in range(SIDES):
        twin_copy(h).wait_send()
    all_of(x_all.at[:, pl.ds(0, RING - 1)], gather_send.at[0], gather_recv.at[0, 0]).wait_send()
    all_of(send_last.at[:, :, pl.ds(1, RING - 1)], last_send.at[0], last_recv.at[0]).wait_send()
    all_of(send_far, far_send.at[0], ring_recv.at[0, 0, 0, 0]).wait_send()
    all_of(send_ring, ring_send.at[0], ring_recv.at[0, 0, 0, 0]).wait_send()

    @pl.when(core == 1)
    def _():
        pairs = x_all.at[:, pl.ds(0, 2 * (RING - 1))]
        all_of(pairs, pair_send.at[0], pair_recv.at[0]).wait_send()


def per_device(features, tiles, places, counts, weight):
    width = features.shape[1]
    slots = tiles.shape[2]
    lanes = width // SIDES
    piece = (SUB, lanes)
    dma = pltpu.SemaphoreType.DMA
    anywhere = pl.BlockSpec(memory_space=pltpu.HBM)
    return pl.pallas_call(
        kernel,
        out_shape=jax.ShapeDtypeStruct(features.shape, BF16),
        in_specs=[anywhere] * 5,
        out_specs=pl.BlockSpec(memory_space=pltpu.VMEM),
        scratch_shapes=[
            pltpu.VMEM((SIDES, 2 * RING, MAST, lanes), BF16),
            pltpu.VMEM((slots + 1, TILE, TILE), BF16),
            pltpu.SMEM((1, slots), jnp.int32),
            pltpu.SMEM((1, 1), jnp.int32),
            pltpu.VMEM(weight.shape, BF16),
            pltpu.VMEM((2, RING, RING, HALF, RING * TILE), BF16),
            pltpu.VMEM((2, RING, SIDES, SUBS) + piece, F32),
            pltpu.VMEM((4, SIDES, SUBS // 2) + piece, BF16),
            pltpu.VMEM((4, SIDES, SUBS // 2) + piece, BF16),
            pltpu.VMEM((4, 3, SIDES, SUBS) + piece, BF16),
            pltpu.VMEM((4, 3, SIDES, SUBS) + piece, BF16),
            pltpu.VMEM((SIDES, 2, RING, HALF, lanes), BF16),
            pltpu.VMEM((SIDES, 2, RING, HALF, lanes), BF16),
            pltpu.VMEM((2, SIDES, HALF, lanes), F32),
            dma((6,)),
            dma((1,)),
            dma((SIDES, RING)),
            dma((1,)),
            dma((SIDES,)),
            dma((SIDES,)),
            dma((SIDES,)),
            dma((1,)),
            dma((1,)),
            dma((4, 3, SIDES, SUBS)),
            dma((1,)),
            dma((SIDES,)),
        ],
        compiler_params=pltpu.CompilerParams(
            collective_id=0, has_side_effects=True, vmem_limit_bytes=55168 * 2**10
        ),
    )(features, tiles, places, counts, weight)


def solution(mesh):
    return jax.shard_map(
        per_device,
        mesh=mesh,
        in_specs=(
            P(("row", "col"), None),
            P("row", "col", None, None, None),
            P("row", "col", None),
            P("row", "col"),
            P(),
        ),
        out_specs=P(("row", "col"), None),
        check_vma=False,
    )
```
